32 devices in a mesh: mem: 2 (over x), tile: 4 (over z), lev: 4 (over y, core).
Axes of the slice: x: 2, y: 2, z: 4, core: 2. Of those that a mesh axis runs over, the one named last changes fastest.
Arguments:
- ensemble: bfloat16 [32, 2, 64, 32768], P(('mem', 'tile'), None, 'lev'), may hold values from -6 to 6
- alpha: bfloat16 [20, 32, 32768], P('lev', ('mem', 'tile')), may hold values from -6 to 6
- vert_root: bfloat16 [64, 20], P('lev'), may hold values from -1.25 to 1.25
- cotangent: bfloat16 [2, 64, 32768], P('mem', 'lev', 'tile'), may hold values from -6 to 6
Outputs:
- increment: bfloat16 [2, 64, 32768], P('mem', 'lev', 'tile')
- alpha_grad: bfloat16 [20, 32, 32768], P('lev', ('mem', 'tile'))
The draws below stay inside these ranges and needn't reach their ends.
All inputs are finite; a program needn't handle non-finite values.
Results may differ from the reference program's by a relative error of at most 0.008.
Values may be sent and summed in bfloat16 or wider, within the bound.
A program may use at most 128 MiB of HBM per device.

```python
import math
import jax
import jax.numpy as jnp
from jax import lax

LEV = 64
MODES = 20
VARS = 2
MEMBERS = 32
CELLS = 32768


def levels(key, extent, split, low, top_value):
    def one(axis_at, shards_of):
        draws = jax.random.uniform(jax.random.fold_in(jax.random.fold_in(key, 6), axis_at), (shards_of,), jnp.float32, low / len(split), top_value / len(split))
        return jnp.repeat(jnp.exp(draws), extent[axis_at] // shards_of).reshape((-1,) + (1,) * (len(extent) - axis_at - 1))

    loudness = one(*split[0])
    for cut in split[1:]:
        loudness = loudness * one(*cut)
    return loudness


def gaussian(key, shape, spread, most, pieces=(), held_as=jnp.bfloat16):
    drawn = jax.random.normal(key, shape, jnp.float32) * spread
    if len(pieces) > 0:
        drawn = levels(key, shape, pieces, -0.22, 0.18) * drawn
    return jnp.clip(drawn, min=-most, max=most).astype(held_as)


def setup_inputs(seed: int = 0) -> dict:
    keys = jax.random.split(jax.random.key(seed), 5)
    return {
        "ensemble": gaussian(keys[0], (MEMBERS, VARS, LEV, CELLS), 1.0, 6.0, ((0, 8), (2, 4))),
        "alpha": gaussian(keys[1], (MODES, MEMBERS, CELLS), 1.0, 6.0, ((0, 4), (1, 8))),
        "vert_root": gaussian(keys[2], (LEV, MODES), MODES ** -0.5, 1.25, ((0, 4),)),
        "cotangent": gaussian(keys[3], (VARS, LEV, CELLS), 1.0, 6.0, ((0, 2), (1, 4), (2, 4))),
    }


def reference(ensemble, alpha, vert_root, cotangent):
    scale = 1.0 / math.sqrt(MEMBERS - 1)
    cot_wide = cotangent.astype(jnp.float32)

    def member(total, items):
        fields, control = items
        lifted = jnp.dot(vert_root, control, preferred_element_type=jnp.float32).astype(jnp.bfloat16)
        fields_wide = fields.astype(jnp.float32)
        total = total + fields_wide * lifted.astype(jnp.float32)[None]
        cross = lax.optimization_barrier(jnp.sum(fields_wide * cot_wide, axis=0)).astype(jnp.bfloat16)
        back = jnp.dot(vert_root.T, cross, preferred_element_type=jnp.float32)
        return (total, (back * scale).astype(jnp.bfloat16))
    start = jnp.zeros((VARS, LEV, CELLS), jnp.float32)
    total, grads = lax.scan(member, start, (ensemble, jnp.moveaxis(alpha, 1, 0)))
    return ((total * scale).astype(jnp.bfloat16), jnp.moveaxis(grads, 0, 1))
```

```python
import functools
import math

import jax
import jax.numpy as jnp
from jax import lax
from jax.experimental import pallas as pl
from jax.experimental.pallas import tpu as pltpu
from jax.sharding import PartitionSpec as P

MEMBERS = 32
MESH = pl.DeviceIdType.MESH
F32 = jnp.float32
BF16 = jnp.bfloat16

CHUNKS = 8
AHEAD = 3
SLOTS = 4
WIDE = 256


def kernel(scale, tiles, levels, ens_ref, alpha_ref, root_ref, cot_ref, inc_ref, grad_ref,
           ens, alpha, cot, lift_w, back_w, keep_c, keep_own, keep_y,
           c1s, c1r, c2s, c2r, d1s, d1r, d2s, d2r,
           ens_sem, own_sem, cot_sem, a_ss, a_rs, bt_ss, bt_rs, bm_ss, bm_rs,
           c1_ss, c1_rs, c2_ss, c2_rs, d1_ss, d1_rs, d2_ss, d2_rs):
    chunks, rows, width = alpha_ref.shape
    members = ens_ref.shape[0]
    modes = root_ref.shape[1] // 4
    pairs = members * tiles
    cells = chunks * width
    mem, tile, lev = lax.axis_index("mem"), lax.axis_index("tile"), lax.axis_index("lev")
    near = {"lev": lev + 1 - 2 * (lev % 2)}
    far = {"lev": (lev + 2) % 4}
    twin = {"mem": 1 - mem}
    tile_to = [{"tile": (tile + i) % tiles} for i in range(tiles)]
    tile_from = [(tile + tiles - i) % tiles for i in range(tiles)]

    def remote(src, dst, ss, rs, to):
        return pltpu.make_async_remote_copy(
            src_ref=src, dst_ref=dst, send_sem=ss, recv_sem=rs, device_id=to, device_id_type=MESH
        )

    def a_far(c):
        return remote(alpha_ref.at[c], alpha.at[c, 2], a_ss.at[c, 0], a_rs.at[c, 0], far)

    def a_near(c):
        return remote(alpha_ref.at[c], alpha.at[c, 1], a_ss.at[c, 1], a_rs.at[c, 1], near)

    def a_pass(c):
        return remote(alpha.at[c, 2], alpha.at[c, 3], a_ss.at[c, 2], a_rs.at[c, 2], near)

    def a_own(c):
        return pltpu.make_async_copy(alpha_ref.at[c], alpha.at[c, 0], own_sem.at[c])

    def b_own(c):
        return pltpu.make_async_copy(cot_ref.at[c], cot.at[c, 0, tile], cot_sem.at[c])

    def b_tile(c, i):
        return remote(cot_ref.at[c], cot.at[c, 0, tile], bt_ss.at[c, i], bt_rs.at[c, i], tile_to[i])

    def b_twin(c, i):
        src = cot_ref.at[c] if i == 0 else cot.at[c, 0, tile_from[i]]
        return remote(src, cot.at[c, 1, tile_from[i]], bm_ss.at[c, i], bm_rs.at[c, i], twin)

    def c_twin(c):
        return remote(c1s.at[c], c1r.at[c], c1_ss.at[c], c1_rs.at[c], twin)

    def c_tile(c, i):
        src = c2s.at[c, (tile + i) % tiles]
        return remote(src, c2r.at[c, i - 1], c2_ss.at[c, i], c2_rs.at[c, i], tile_to[i])

    def d_near(c):
        return remote(d1s.at[c], d1r.at[c], d1_ss.at[c], d1_rs.at[c], near)

    def d_far(c):
        return remote(d2s.at[c], d2r.at[c], d2_ss.at[c], d2_rs.at[c], far)

    def e_load(c, t):
        src = ens_ref.at[:, :, :, pl.ds(pl.multiple_of(t * cells + c * width, width), width)]
        return pltpu.make_async_copy(src, ens.at[c % SLOTS, t], ens_sem.at[c % SLOTS, t])

    def first_sends(c):
        a_far(c).start()
        for i in range(1, tiles):
            b_tile(c, i).start()
        b_twin(c, 0).start()
        a_near(c).start()
        a_own(c).start()
        b_own(c).start()

    barrier = pltpu.get_barrier_semaphore()
    greeted = [near, far, twin] + tile_to[1:]
    for other in greeted:
        pl.semaphore_signal(barrier, inc=1, device_id=other, device_id_type=MESH)
    for c in range(min(2, chunks)):
        for t in range(tiles):
            e_load(c, t).start()
    pl.semaphore_wait(barrier, len(greeted))

    @pl.loop(0, min(AHEAD, chunks))
    def _(c):
        first_sends(c)

    def mode_of(j):
        r = jnp.where(j >= modes, 1, 0) + jnp.where(j >= 2 * modes, 1, 0) + jnp.where(j >= 3 * modes, 1, 0)
        home = jnp.where(
            r == 0, lev, jnp.where(r == 1, near["lev"], jnp.where(r == 2, far["lev"], 3 - lev))
        )
        return home * modes + (j - r * modes)

    def hot(mask):
        return jnp.where(mask, 1.0, 0.0).astype(BF16)

    def iota(shape, axis):
        return lax.broadcasted_iota(jnp.int32, shape, axis)

    high, deep = pairs * levels, 4 * rows
    root = root_ref[...]
    by_level = hot(iota((high, levels), 0) % levels == iota((high, levels), 1))
    by_mode = hot(mode_of(iota((4 * modes, deep), 1) // pairs) == iota((4 * modes, deep), 0))
    spread = jnp.dot(by_level, root, preferred_element_type=F32).astype(BF16)
    spread = jnp.dot(spread, by_mode, preferred_element_type=F32)
    same = iota((high, deep), 0) // levels == iota((high, deep), 1) % pairs
    lift_w[...] = jnp.where(same, spread, 0.0).astype(BF16)
    by_mode_t = hot(mode_of(iota((deep, 4 * modes), 0) // pairs) == iota((deep, 4 * modes), 1))
    by_level_t = hot(iota((levels, high), 1) % levels == iota((levels, high), 0))
    spread_t = lax.dot_general(
        by_mode_t, root, (((1,), (1,)), ((), ())), preferred_element_type=F32
    ).astype(BF16)
    spread_t = jnp.dot(spread_t, by_level_t, preferred_element_type=F32)
    same_t = iota((deep, high), 1) // levels == iota((deep, high), 0) % pairs
    back_w[...] = jnp.where(same_t, spread_t, 0.0).astype(BF16)

    def compute_adjoint(c):
        e, slot = c % SLOTS, c % SLOTS

        @pl.loop(0, width // WIDE)
        def _(j):
            cols = pl.ds(pl.multiple_of(j * WIDE, WIDE), WIDE)
            own = [cot[c, 0, t, :, cols].astype(F32) for t in range(tiles)]
            other = [cot[c, 1, t, :, cols].astype(F32) for t in range(tiles)]
            cross = jnp.concatenate(
                [
                    (
                        ens[e, t, k, mem, :, cols].astype(F32) * own[t]
                        + ens[e, t, k, 1 - mem, :, cols].astype(F32) * other[t]
                    ).astype(BF16)
                    for k in range(members)
                    for t in range(tiles)
                ],
                axis=0,
            )
            back = jnp.dot(back_w[...], cross, preferred_element_type=F32)
            keep_own[slot, :, cols] = back[:rows]
            d1s[c, 0, :, cols] = back[rows : 2 * rows].astype(BF16)
            keep_y[slot, :, cols] = back[2 * rows : 3 * rows]
            d1s[c, 1, :, cols] = back[3 * rows :].astype(BF16)

    def compute_lift(c):
        e, slot = c % SLOTS, c % SLOTS

        @pl.loop(0, width // WIDE)
        def _(j):
            cols = pl.ds(pl.multiple_of(j * WIDE, WIDE), WIDE)
            fields = alpha[c, :, :, cols].reshape(deep, WIDE)
            lifted = jnp.dot(lift_w[...], fields, preferred_element_type=F32)
            lifted = lifted.astype(BF16).astype(F32)
            for t in range(tiles):
                own = other = None
                for k in range(members):
                    at = (k * tiles + t) * levels
                    part = lifted[at : at + levels]
                    one = ens[e, t, k, mem, :, cols].astype(F32) * part
                    two = ens[e, t, k, 1 - mem, :, cols].astype(F32) * part
                    own = one if own is None else own + one
                    other = two if other is None else other + two
                keep_c[slot, t, :, cols] = own
                c1s[c, t, :, cols] = other.astype(BF16)

    @pl.loop(0, chunks + 3)
    def _(step):
        @pl.when(step < chunks)
        def _():
            c = step

            @pl.when(c + AHEAD < chunks)
            def _():
                first_sends(c + AHEAD)

            @pl.when(c + 2 < chunks)
            def _():
                for t in range(tiles):
                    e_load(c + 2, t).start()

            for i in range(1, tiles):
                b_tile(c, i).wait_recv()
                b_twin(c, i).start()
            a_far(c).wait_recv()
            a_pass(c).start()

        @pl.when((step >= 1) & (step <= chunks))
        def _():
            c = step - 1
            for t in range(tiles):
                e_load(c, t).wait()
            b_own(c).wait()
            for i in range(tiles):
                b_twin(c, i).wait_recv()
            compute_adjoint(c)
            d_near(c).start()
            a_own(c).wait()
            a_near(c).wait_recv()
            a_pass(c).wait_recv()
            compute_lift(c)
            c_twin(c).start()
            d_near(c).wait_recv()
            slot = c % SLOTS
            d2s[c] = (keep_y[slot] + d1r[c, 1].astype(F32)).astype(BF16)
            d_far(c).start()
            keep_own[slot] = keep_own[slot] + d1r[c, 0].astype(F32)

        @pl.when((step >= 2) & (step <= chunks + 1))
        def _():
            c = step - 2
            slot = c % SLOTS
            c_twin(c).wait_recv()
            for t in range(tiles):
                total = keep_c[slot, t] + c1r[c, t].astype(F32)
                keep_c[slot, t] = total
                c2s[c, t] = total.astype(BF16)
            for i in range(1, tiles):
                c_tile(c, i).start()

        @pl.when(step >= 3)
        def _():
            c = step - 3
            slot = c % SLOTS
            total = keep_c[slot, tile]
            for i in range(1, tiles):
                c_tile(c, i).wait_recv()
                total = total + c2r[c, i - 1].astype(F32)
            inc_ref[:, pl.ds(pl.multiple_of(c * width, width), width)] = (total * scale).astype(BF16)
            d_far(c).wait_recv()
            grad_ref[c] = ((keep_own[slot] + d2r[c].astype(F32)) * scale).astype(BF16)

    @pl.loop(0, chunks)
    def _(c):
        a_far(c).wait_send()
        a_near(c).wait_send()
        a_pass(c).wait_send()
        b_twin(c, 0).wait_send()
        for i in range(1, tiles):
            b_tile(c, i).wait_send()
            b_twin(c, i).wait_send()
            c_tile(c, i).wait_send()
        c_twin(c).wait_send()
        d_near(c).wait_send()
        d_far(c).wait_send()


def on_device(tiles, ensemble, alpha, vert_root, cotangent):
    scale = 1.0 / math.sqrt(MEMBERS - 1)
    members, _, levels, whole = ensemble.shape
    modes = alpha.shape[0]
    cells = whole // tiles
    chunks, width = CHUNKS, cells // CHUNKS
    rows = modes * members * tiles
    packed = alpha.reshape(modes, members, tiles, chunks, width)
    packed = packed.transpose(3, 0, 1, 2, 4).reshape(chunks, rows, width)
    cot = cotangent.reshape(levels, chunks, width).transpose(1, 0, 2)
    vmem, dma = pltpu.VMEM, pltpu.SemaphoreType.DMA
    sums = (chunks, tiles, levels, width)
    increment, grad = pl.pallas_call(
        functools.partial(kernel, scale, tiles, levels),
        out_shape=(
            jax.ShapeDtypeStruct((levels, cells), BF16),
            jax.ShapeDtypeStruct((chunks, rows, width), BF16),
        ),
        in_specs=[
            pl.BlockSpec(memory_space=pl.ANY),
            pl.BlockSpec(memory_space=pl.ANY),
            pl.BlockSpec(memory_space=pltpu.VMEM),
            pl.BlockSpec(memory_space=pl.ANY),
        ],
        out_specs=(pl.BlockSpec(memory_space=pltpu.VMEM), pl.BlockSpec(memory_space=pltpu.VMEM)),
        scratch_shapes=[
            vmem((SLOTS, tiles, members, 2, levels, width), BF16),
            vmem((chunks, 4, rows, width), BF16),
            vmem((chunks, 2, tiles, levels, width), BF16),
            vmem((members * tiles * levels, 4 * rows), BF16),
            vmem((4 * rows, members * tiles * levels), BF16),
            vmem((SLOTS, tiles, levels, width), F32),
            vmem((SLOTS, rows, width), F32),
            vmem((SLOTS, rows, width), F32),
            vmem(sums, BF16),
            vmem(sums, BF16),
            vmem(sums, BF16),
            vmem((chunks, tiles - 1, levels, width), BF16),
            vmem((chunks, 2, rows, width), BF16),
            vmem((chunks, 2, rows, width), BF16),
            vmem((chunks, rows, width), BF16),
            vmem((chunks, rows, width), BF16),
            dma((SLOTS, tiles)),
            dma((chunks,)),
            dma((chunks,)),
            dma((chunks, 3)),
            dma((chunks, 3)),
            dma((chunks, tiles)),
            dma((chunks, tiles)),
            dma((chunks, tiles)),
            dma((chunks, tiles)),
            dma((chunks,)),
            dma((chunks,)),
            dma((chunks, tiles)),
            dma((chunks, tiles)),
            dma((chunks,)),
            dma((chunks,)),
            dma((chunks,)),
            dma((chunks,)),
        ],
        compiler_params=pltpu.CompilerParams(
            collective_id=0, has_side_effects=True, vmem_limit_bytes=60 * 1024 * 1024
        ),
    )(ensemble, packed, vert_root, cot)
    grad = grad.reshape(chunks, modes, members, tiles, width).transpose(1, 2, 3, 0, 4)
    return increment[None], grad.reshape(modes, members, whole)


def solution(mesh):
    in_specs = (
        P(("mem", "tile"), None, "lev", None),
        P("lev", ("mem", "tile"), None),
        P("lev", None),
        P("mem", "lev", "tile"),
    )
    out_specs = (P("mem", "lev", "tile"), P("lev", ("mem", "tile"), None))
    return jax.shard_map(
        functools.partial(on_device, mesh.shape["tile"]),
        mesh=mesh, in_specs=in_specs, out_specs=out_specs, check_vma=False,
    )
```

```python
import functools
import math

import jax
import jax.numpy as jnp
from jax import lax
from jax.experimental import pallas as pl
from jax.experimental.pallas import tpu as pltpu
from jax.sharding import PartitionSpec as P

MEMBERS = 32
MESH = pl.DeviceIdType.MESH
F32 = jnp.float32
BF16 = jnp.bfloat16

CHUNKS = 8
AHEAD = 3
SLOTS = 4
WIDE = 256


def kernel(scale, tiles, levels, ens_ref, alpha_ref, root_ref, cot_ref, inc_ref, grad_ref,
           ens, alpha, cot, lift_w, back_w, keep_c, keep_own, keep_y,
           c1s, c1r, c2s, c2r, d1s, d1r, d2s, d2r,
           ens_sem, cot_sem, a_ss, a_rs, bt_ss, bt_rs, bm_ss, bm_rs,
           c1_ss, c1_rs, c2_ss, c2_rs, d1_ss, d1_rs, d2_ss, d2_rs):
    chunks, _, rows, width = alpha.shape
    modes, members, _ = alpha_ref.shape
    pairs = members * tiles
    cells = chunks * width
    mem, tile, lev = lax.axis_index("mem"), lax.axis_index("tile"), lax.axis_index("lev")
    near = {"lev": lev + 1 - 2 * (lev % 2)}
    far = {"lev": (lev + 2) % 4}
    twin = {"mem": 1 - mem}
    tile_to = [{"tile": (tile + i) % tiles} for i in range(tiles)]
    tile_from = [(tile + tiles - i) % tiles for i in range(tiles)]

    def remote(src, dst, ss, rs, to):
        return pltpu.make_async_remote_copy(
            src_ref=src, dst_ref=dst, send_sem=ss, recv_sem=rs, device_id=to, device_id_type=MESH
        )

    def a_far(c):
        return remote(alpha.at[c, 0], alpha.at[c, 2], a_ss.at[c, 0], a_rs.at[c, 0], far)

    def a_near(c):
        return remote(alpha.at[c, 0], alpha.at[c, 1], a_ss.at[c, 1], a_rs.at[c, 1], near)

    def a_pass(c):
        return remote(alpha.at[c, 2], alpha.at[c, 3], a_ss.at[c, 2], a_rs.at[c, 2], near)

    def place(c, t):
        return pl.ds(pl.multiple_of(t * cells + c * width, width), width)

    def pack(c):
        for m in range(modes):
            pieces = [alpha_ref[m, :, place(c, t)].astype(F32) for t in range(tiles)]
            alpha[c, 0, m * pairs : (m + 1) * pairs, :] = jnp.concatenate(pieces, axis=0).astype(BF16)

    def b_own(c):
        return pltpu.make_async_copy(cot_ref.at[:, place(c, 0)], cot.at[c, 0, tile], cot_sem.at[c])

    def b_tile(c, i):
        return remote(cot_ref.at[:, place(c, 0)], cot.at[c, 0, tile], bt_ss.at[c, i], bt_rs.at[c, i], tile_to[i])

    def b_twin(c, i):
        src = cot_ref.at[:, place(c, 0)] if i == 0 else cot.at[c, 0, tile_from[i]]
        return remote(src, cot.at[c, 1, tile_from[i]], bm_ss.at[c, i], bm_rs.at[c, i], twin)

    def c_twin(c):
        return remote(c1s.at[c], c1r.at[c], c1_ss.at[c], c1_rs.at[c], twin)

    def c_tile(c, i):
        src = c2s.at[c, (tile + i) % tiles]
        return remote(src, c2r.at[c, i - 1], c2_ss.at[c, i], c2_rs.at[c, i], tile_to[i])

    def d_near(c):
        return remote(d1s.at[c], d1r.at[c], d1_ss.at[c], d1_rs.at[c], near)

    def d_far(c):
        return remote(d2s.at[c], d2r.at[c], d2_ss.at[c], d2_rs.at[c], far)

    def e_load(c, t):
        src = ens_ref.at[:, :, :, place(c, t)]
        return pltpu.make_async_copy(src, ens.at[c % SLOTS, t], ens_sem.at[c % SLOTS, t])

    def first_sends(c):
        for i in range(1, tiles):
            b_tile(c, i).start()
        b_twin(c, 0).start()
        pack(c)
        a_far(c).start()
        a_near(c).start()
        b_own(c).start()

    barrier = pltpu.get_barrier_semaphore()
    greeted = [near, far, twin] + tile_to[1:]
    for other in greeted:
        pl.semaphore_signal(barrier, inc=1, device_id=other, device_id_type=MESH)
    for c in range(min(2, chunks)):
        for t in range(tiles):
            e_load(c, t).start()
    pl.semaphore_wait(barrier, len(greeted))

    @pl.loop(0, min(AHEAD, chunks))
    def _(c):
        first_sends(c)

    def mode_of(j):
        r = jnp.where(j >= modes, 1, 0) + jnp.where(j >= 2 * modes, 1, 0) + jnp.where(j >= 3 * modes, 1, 0)
        home = jnp.where(
            r == 0, lev, jnp.where(r == 1, near["lev"], jnp.where(r == 2, far["lev"], 3 - lev))
        )
        return home * modes + (j - r * modes)

    def hot(mask):
        return jnp.where(mask, 1.0, 0.0).astype(BF16)

    def iota(shape, axis):
        return lax.broadcasted_iota(jnp.int32, shape, axis)

    high, deep = pairs * levels, 4 * rows
    root = root_ref[...]
    by_level = hot(iota((high, levels), 0) % levels == iota((high, levels), 1))
    by_mode = hot(mode_of(iota((4 * modes, deep), 1) // pairs) == iota((4 * modes, deep), 0))
    spread = jnp.dot(by_level, root, preferred_element_type=F32).astype(BF16)
    spread = jnp.dot(spread, by_mode, preferred_element_type=F32)
    same = iota((high, deep), 0) // levels == iota((high, deep), 1) % pairs
    lift_w[...] = jnp.where(same, spread, 0.0).astype(BF16)
    by_mode_t = hot(mode_of(iota((deep, 4 * modes), 0) // pairs) == iota((deep, 4 * modes), 1))
    by_level_t = hot(iota((levels, high), 1) % levels == iota((levels, high), 0))
    spread_t = lax.dot_general(
        by_mode_t, root, (((1,), (1,)), ((), ())), preferred_element_type=F32
    ).astype(BF16)
    spread_t = jnp.dot(spread_t, by_level_t, preferred_element_type=F32)
    same_t = iota((deep, high), 1) // levels == iota((deep, high), 0) % pairs
    back_w[...] = jnp.where(same_t, spread_t, 0.0).astype(BF16)

    def compute_adjoint(c):
        e, slot = c % SLOTS, c % SLOTS

        @pl.loop(0, width // WIDE)
        def _(j):
            cols = pl.ds(pl.multiple_of(j * WIDE, WIDE), WIDE)
            own = [cot[c, 0, t, :, cols].astype(F32) for t in range(tiles)]
            other = [cot[c, 1, t, :, cols].astype(F32) for t in range(tiles)]
            cross = jnp.concatenate(
                [
                    (
                        ens[e, t, k, mem, :, cols].astype(F32) * own[t]
                        + ens[e, t, k, 1 - mem, :, cols].astype(F32) * other[t]
                    ).astype(BF16)
                    for t in range(tiles)
                    for k in range(members)
                ],
                axis=0,
            )
            back = jnp.dot(back_w[...], cross, preferred_element_type=F32)
            keep_own[slot, :, cols] = back[:rows]
            d1s[c, 0, :, cols] = back[rows : 2 * rows].astype(BF16)
            keep_y[slot, :, cols] = back[2 * rows : 3 * rows]
            d1s[c, 1, :, cols] = back[3 * rows :].astype(BF16)

    def compute_lift(c):
        e, slot = c % SLOTS, c % SLOTS

        @pl.loop(0, width // WIDE)
        def _(j):
            cols = pl.ds(pl.multiple_of(j * WIDE, WIDE), WIDE)
            fields = alpha[c, :, :, cols].reshape(deep, WIDE)
            lifted = jnp.dot(lift_w[...], fields, preferred_element_type=F32)
            lifted = lifted.astype(BF16).astype(F32)
            for t in range(tiles):
                own = other = None
                for k in range(members):
                    at = (t * members + k) * levels
                    part = lifted[at : at + levels]
                    one = ens[e, t, k, mem, :, cols].astype(F32) * part
                    two = ens[e, t, k, 1 - mem, :, cols].astype(F32) * part
                    own = one if own is None else own + one
                    other = two if other is None else other + two
                keep_c[slot, t, :, cols] = own
                c1s[c, t, :, cols] = other.astype(BF16)

    @pl.loop(0, chunks + 3)
    def _(step):
        @pl.when(step < chunks)
        def _():
            c = step

            @pl.when(c + AHEAD < chunks)
            def _():
                first_sends(c + AHEAD)

            @pl.when(c + 2 < chunks)
            def _():
                for t in range(tiles):
                    e_load(c + 2, t).start()

            for i in range(1, tiles):
                b_tile(c, i).wait_recv()
                b_twin(c, i).start()
            a_far(c).wait_recv()
            a_pass(c).start()

        @pl.when((step >= 1) & (step <= chunks))
        def _():
            c = step - 1
            for t in range(tiles):
                e_load(c, t).wait()
            b_own(c).wait()
            for i in range(tiles):
                b_twin(c, i).wait_recv()
            compute_adjoint(c)
            d_near(c).start()
            a_near(c).wait_recv()
            a_pass(c).wait_recv()
            compute_lift(c)
            c_twin(c).start()
            d_near(c).wait_recv()
            slot = c % SLOTS
            d2s[c] = (keep_y[slot] + d1r[c, 1].astype(F32)).astype(BF16)
            d_far(c).start()
            keep_own[slot] = keep_own[slot] + d1r[c, 0].astype(F32)

        @pl.when((step >= 2) & (step <= chunks + 1))
        def _():
            c = step - 2
            slot = c % SLOTS
            c_twin(c).wait_recv()
            for t in range(tiles):
                total = keep_c[slot, t] + c1r[c, t].astype(F32)
                keep_c[slot, t] = total
                c2s[c, t] = total.astype(BF16)
            for i in range(1, tiles):
                c_tile(c, i).start()

        @pl.when(step >= 3)
        def _():
            c = step - 3
            slot = c % SLOTS
            total = keep_c[slot, tile]
            for i in range(1, tiles):
                c_tile(c, i).wait_recv()
                total = total + c2r[c, i - 1].astype(F32)
            inc_ref[:, place(c, 0)] = (total * scale).astype(BF16)
            d_far(c).wait_recv()
            for m in range(modes):
                at = slice(m * pairs, (m + 1) * pairs)
                done = (keep_own[slot, at] + d2r[c, at].astype(F32)) * scale
                for t in range(tiles):
                    part = done[t * members : (t + 1) * members]
                    grad_ref[m, :, place(c, t)] = part.astype(BF16)

    @pl.loop(0, chunks)
    def _(c):
        a_far(c).wait_send()
        a_near(c).wait_send()
        a_pass(c).wait_send()
        b_twin(c, 0).wait_send()
        for i in range(1, tiles):
            b_tile(c, i).wait_send()
            b_twin(c, i).wait_send()
            c_tile(c, i).wait_send()
        c_twin(c).wait_send()
        d_near(c).wait_send()
        d_far(c).wait_send()


def on_device(tiles, ensemble, alpha, vert_root, cotangent):
    scale = 1.0 / math.sqrt(MEMBERS - 1)
    members, _, levels, whole = ensemble.shape
    modes = alpha.shape[0]
    cells = whole // tiles
    chunks, width = CHUNKS, cells // CHUNKS
    rows = modes * members * tiles
    vmem, dma = pltpu.VMEM, pltpu.SemaphoreType.DMA
    sums = (chunks, tiles, levels, width)
    increment, grad = pl.pallas_call(
        functools.partial(kernel, scale, tiles, levels),
        out_shape=(
            jax.ShapeDtypeStruct((levels, cells), BF16),
            jax.ShapeDtypeStruct(alpha.shape, BF16),
        ),
        in_specs=[
            pl.BlockSpec(memory_space=pl.ANY),
            pl.BlockSpec(memory_space=pltpu.VMEM),
            pl.BlockSpec(memory_space=pltpu.VMEM),
            pl.BlockSpec(memory_space=pl.ANY),
        ],
        out_specs=(pl.BlockSpec(memory_space=pltpu.VMEM), pl.BlockSpec(memory_space=pltpu.VMEM)),
        scratch_shapes=[
            vmem((SLOTS, tiles, members, 2, levels, width), BF16),
            vmem((chunks, 4, rows, width), BF16),
            vmem((chunks, 2, tiles, levels, width), BF16),
            vmem((members * tiles * levels, 4 * rows), BF16),
            vmem((4 * rows, members * tiles * levels), BF16),
            vmem((SLOTS, tiles, levels, width), F32),
            vmem((SLOTS, rows, width), F32),
            vmem((SLOTS, rows, width), F32),
            vmem(sums, BF16),
            vmem(sums, BF16),
            vmem(sums, BF16),
            vmem((chunks, tiles - 1, levels, width), BF16),
            vmem((chunks, 2, rows, width), BF16),
            vmem((chunks, 2, rows, width), BF16),
            vmem((chunks, rows, width), BF16),
            vmem((chunks, rows, width), BF16),
            dma((SLOTS, tiles)),
            dma((chunks,)),
            dma((chunks, 3)),
            dma((chunks, 3)),
            dma((chunks, tiles)),
            dma((chunks, tiles)),
            dma((chunks, tiles)),
            dma((chunks, tiles)),
            dma((chunks,)),
            dma((chunks,)),
            dma((chunks, tiles)),
            dma((chunks, tiles)),
            dma((chunks,)),
            dma((chunks,)),
            dma((chunks,)),
            dma((chunks,)),
        ],
        compiler_params=pltpu.CompilerParams(
            collective_id=0, has_side_effects=True, vmem_limit_bytes=60 * 1024 * 1024
        ),
    )(ensemble, alpha, vert_root, cotangent.reshape(levels, cells))
    return increment[None], grad


def solution(mesh):
    in_specs = (
        P(("mem", "tile"), None, "lev", None),
        P("lev", ("mem", "tile"), None),
        P("lev", None),
        P("mem", "lev", "tile"),
    )
    out_specs = (P("mem", "lev", "tile"), P("lev", ("mem", "tile"), None))
    return jax.shard_map(
        functools.partial(on_device, mesh.shape["tile"]),
        mesh=mesh, in_specs=in_specs, out_specs=out_specs, check_vma=False,
    )
```
